256 devices in a mesh: pair: 64 (over y, z, core), virt: 4 (over x).
Axes of the slice: x: 4, y: 4, z: 8, core: 2. Of those that a mesh axis runs over, the one named last changes fastest.
Arguments:
- amplitudes: bfloat16 [256, 256, 8, 128], P('pair', None, 'virt'), may hold values from -6 to 6
- amp_ids: int32 [256, 16, 8], P('pair', None, 'virt'), may hold values from 0 to 16, as said below
- integrals: bfloat16 [64, 1024, 128], P('virt', 'pair'), may hold values from -0.375 to 0.375
- int_ids: int32 [64, 8], P('virt'), may hold values from 0 to 15, as said below
Outputs:
- symmetrized: bfloat16 [256, 256, 8192], P('pair', None, 'virt')
The draws below stay inside these ranges and needn't reach their ends.
Inputs may be any that keep to these rules, and one draw needn't show every extreme that they name: `amp_ids`: in each amplitude tile the live slots come first and name distinct tiles; the remaining slots hold 16; a tile has 4 to 8 live slots, both ends reached. `int_ids`: the 8 tiles listed for one column tile are distinct.
All inputs are finite; a program needn't handle non-finite values.
Results may differ from the reference program's by a relative error of at most 0.0052.
Values may be sent and summed in bfloat16 or wider, within the bound.
No kernel may reach another device: no remote copies, remote signals or barrier semaphores. Data moves between devices by JAX's collectives and lax.ppermute only.
A program may use at most 320 MiB of HBM per device.

```python
import jax
import jax.numpy as jnp
from jax import lax

VB = 128
OJ = 16
NK = 16
NZT = 8
NZV = 8
NOCC = 256
NCOL = 64


def permuted(key, count, shape_out):
    scores = jax.random.randint(key, shape_out + (NK,), 0, 1 << 20) * NK + jnp.arange(NK, dtype=jnp.int32)
    return jnp.argsort(scores, axis=-1)[..., :count].astype(jnp.int32)


def draw_amp_ids(key, part):
    key = jax.random.fold_in(key, 5)
    first, second = jax.random.split(key)
    ordering = permuted(first, NZT, (NOCC, NOCC // OJ))
    live_count = jax.random.randint(second, (NOCC, NOCC // OJ, 1), NZT // 2, NZT + 1)
    live_count = live_count.at[0, 0, 0].set(NZT).at[-1, -1, 0].set(NZT // 2)
    slot_index = jnp.arange(NZT, dtype=jnp.int32)
    return jnp.where(slot_index < live_count, ordering, NK).astype(jnp.int32)


def draw_int_ids(key, part):
    key = jax.random.fold_in(key, 9)
    ordering = permuted(key, NZV, (NCOL,))
    highest = NK - 1 - jnp.arange(NZV, dtype=jnp.int32)
    return ordering.at[0].set(highest).astype(jnp.int32)


def steps_of(key, shape, cuts, smallest, largest):
    gain = 1.0
    for axis_at, parts in cuts:
        draws = jax.random.uniform(jax.random.fold_in(jax.random.fold_in(key, 6), axis_at), (parts,), jnp.float32, smallest / len(cuts), largest / len(cuts))
        gain = gain * jnp.repeat(jnp.exp(draws), shape[axis_at] // parts).reshape((-1,) + (1,) * (len(shape) - 1 - axis_at))
    return gain


def centred(stream_key, extent, spread, limit, cuts=(), held_as=jnp.bfloat16):
    result = jax.random.normal(stream_key, extent, jnp.float32) * spread
    if len(cuts) > 0:
        result = steps_of(stream_key, extent, cuts, -0.22, 0.18) * result
    return jnp.clip(result, min=-limit, max=limit).astype(held_as)


def setup_inputs(seed: int = 0) -> dict:
    seeds = jax.random.split(jax.random.key(seed), 5)
    amplitudes = centred(seeds[0], (NOCC, NOCC, NZT, VB), 1.0, 6.0, ((0, 64), (2, 4)))
    amp_ids = draw_amp_ids(jax.random.fold_in(seeds[4], 71), 0)
    integrals = centred(seeds[2], (NCOL, NZV * VB, VB), (2 * VB) ** -0.5, 0.375, ((0, 4), (1, 64)))
    int_ids = draw_int_ids(jax.random.fold_in(seeds[4], 71), 0)
    return {"amplitudes": amplitudes, "amp_ids": amp_ids, "integrals": integrals, "int_ids": int_ids}


def mirror_columns(values):
    tile_width = VB
    sub_rows = tile_width // 16
    shape_in = values.shape
    blocks = values.reshape(shape_in[:-1] + (shape_in[-1] // (2 * tile_width), 2, tile_width))
    even_part = blocks[..., 0, :]
    odd_part = blocks[..., 1, :]
    new_even = jnp.swapaxes(odd_part.reshape(odd_part.shape[:-1] + (16, sub_rows)), -1, -2).reshape(odd_part.shape)
    new_odd = jnp.swapaxes(even_part.reshape(even_part.shape[:-1] + (sub_rows, 16)), -1, -2).reshape(even_part.shape)
    return jnp.stack([new_even, new_odd], axis=-2).reshape(shape_in)


def densify_row(block, slot_ids):
    onehot = (slot_ids[:, :, None] == jnp.arange(NK, dtype=jnp.int32)[None, None, :]).astype(jnp.float32)
    return jnp.einsum("jsk,jsc->jkc", onehot, block.astype(jnp.float32))


def reference(amplitudes, amp_ids, integrals, int_ids):
    row_ids = jnp.repeat(amp_ids, OJ, axis=1)
    flat_ids = int_ids.reshape(-1).astype(jnp.int32)
    weights = integrals.astype(jnp.float32)

    def one_row(pair_data):
        block, slot_ids = pair_data
        dense_part = densify_row(block, slot_ids)
        selected = jnp.take(dense_part, flat_ids, axis=1).reshape(NOCC, NCOL, NZV * VB)
        product = jnp.einsum("jbk,bkc->jbc", selected, weights)
        return product.reshape(NOCC, NCOL * VB).astype(jnp.bfloat16)

    ladder = lax.map(one_row, (amplitudes, row_ids))
    swapped = jnp.transpose(ladder, (1, 0, 2))
    total = ladder.astype(jnp.float32) + mirror_columns(swapped).astype(jnp.float32)
    return total.astype(jnp.bfloat16)
```

```python
import functools

import jax
import jax.numpy as jnp
import numpy as np
from jax import lax
from jax.experimental import pallas as pl
from jax.experimental.pallas import tpu as pltpu
from jax.sharding import PartitionSpec as P

VB = 128
OJ = 16
NK = 16
NY, NZ, NC, NX = 4, 8, 2, 4
BF = jnp.bfloat16
F32 = jnp.float32


def position(y, z, c):
    return ((y % NY) * NZ + z % NZ) * NC + c % NC


def pair_shift(dy, dz, dc):
    return [
        (position(y, z, c), position(y + dy, z + dz, c + dc))
        for y in range(NY)
        for z in range(NZ)
        for c in range(NC)
    ]


def virt_gather(block):
    shifts = (1, NX - 1, 2)
    return [block] + [
        lax.ppermute(block, "virt", [(x, (x + k) % NX) for x in range(NX)]) for k in shifts
    ]


def mirror_matrices():
    matrix = np.zeros((2, VB, VB), np.float32)
    for a in range(VB // 16):
        for e in range(16):
            matrix[0, a * 16 + e, e * (VB // 16) + a] = 1.0
            matrix[1, e * (VB // 16) + a, a * 16 + e] = 1.0
    return matrix


def own_kernel(amp_ids, int_ids, place, s0, s1, s2, s3, *rest):
    blocks, (mirror, ladder, mirrored, amps, dense, listed) = rest[:8], rest[8:]
    step = pl.program_id(0)
    rows = amps.shape[0]
    shards = (s0, s1, s2, s3)

    @pl.when(step == 0)
    def _():
        def clear(t, carry):
            amps[pl.ds(t * 64, 64), :] = jnp.zeros((64, amps.shape[1]), BF)
            return carry

        lax.fori_loop(0, rows // 64, clear, 0)

        def place_tile(t, carry):
            i, jt = t // 16, t % 16
            row = pl.multiple_of(t * OJ, OJ)
            for n, shard in enumerate(shards):
                for s in range(2):
                    k = amp_ids[n, t * 2 + s]
                    source = pl.multiple_of((i * 2 + s) * 256 + jt * OJ, OJ)
                    amps[pl.ds(row, OJ), pl.ds(pl.multiple_of(k * VB, VB), VB)] = shard[
                        pl.ds(source, OJ), :
                    ]
            return carry

        lax.fori_loop(0, rows // OJ, place_tile, 0)

    dense[...] = jnp.zeros(dense.shape, BF)
    mirrored[...] = jnp.zeros(mirrored.shape, BF)
    for half in range(2):
        b = step * 2 + half
        for n in range(4):
            for core in range(2):
                block = blocks[n * 2 + core]
                c = place[4] if core == 0 else 1 - place[4]
                base = place[n] * 256 + c * OJ
                for z in range(NZ):
                    listed[pl.ds(pl.multiple_of(base + z * 32, OJ), OJ), :] = block[z, half]
        turned = jnp.dot(listed[...], mirror[half], preferred_element_type=F32).astype(BF)
        for v in range(8):
            k = pl.multiple_of(int_ids[b, v] * VB, VB)
            dense[pl.ds(k, VB), pl.ds(half * VB, VB)] = listed[pl.ds(v * VB, VB), :]
            mirrored[pl.ds(k, VB), pl.ds((1 - half) * VB, VB)] = turned[v * VB : (v + 1) * VB]
    for m in range(2):
        part = pl.ds(m * (rows // 2), rows // 2)
        ladder[part, :] = jnp.dot(
            amps[part, : NK * VB], dense[...], preferred_element_type=F32
        ).astype(BF)


def own_ladder(amp_ids, int_ids, place, shards, blocks, mirror):
    rows, pairs = 1024, 8
    shard_spec = pl.BlockSpec((shards[0].shape[0], VB), lambda p: (0, 0))
    block_spec = pl.BlockSpec((NZ, 2, OJ, VB), lambda p: (0, p, 0, 0))
    smem = pl.BlockSpec(memory_space=pltpu.SMEM)
    return pl.pallas_call(
        own_kernel,
        grid=(pairs,),
        in_specs=[smem] * 3
        + [shard_spec] * 4
        + [block_spec] * 8
        + [pl.BlockSpec((2, VB, VB), lambda p: (0, 0, 0))],
        out_specs=[
            pl.BlockSpec((rows, 2 * VB), lambda p: (0, p)),
            pl.BlockSpec((NK * VB, 2 * VB), lambda p: (0, p)),
        ],
        out_shape=[
            jax.ShapeDtypeStruct((rows, pairs * 2 * VB), BF),
            jax.ShapeDtypeStruct((NK * VB, pairs * 2 * VB), BF),
        ],
        scratch_shapes=[
            pltpu.VMEM((rows, (NK + 1) * VB), BF),
            pltpu.VMEM((NK * VB, 2 * VB), BF),
            pltpu.VMEM((8 * VB, VB), BF),
        ],
        compiler_params=pltpu.CompilerParams(vmem_limit_bytes=48 * 2**20),
        cost_estimate=pl.CostEstimate(flops=9 * 10**9, bytes_accessed=24 * 2**20, transcendentals=0),
        name="own_ladder",
    )(amp_ids, int_ids, place, *shards, *blocks, mirror)


def turn_kernel(ids, s0, s1, s2, s3, mirrored, ladder, *rest):
    out, amps = rest[-2:]
    shards = (s0, s1, s2, s3)

    @pl.when(pl.program_id(0) == 0)
    def _():
        def place_rows(t, carry):
            row = pl.multiple_of(t * OJ, OJ)
            slots = [
                jnp.broadcast_to(ids[pl.ds(row, OJ), n : n + 1], (OJ, VB)).astype(BF)
                for n in range(8)
            ]
            for i in range(2):
                values = [
                    shards[n // 2][pl.ds(pl.multiple_of((i * 2 + n % 2) * 256 + row, OJ), OJ), :]
                    for n in range(8)
                ]
                for k in range(NK):
                    total = jnp.zeros((OJ, VB), BF)
                    for n in range(8):
                        total = jnp.where(slots[n] == BF(k), values[n], total)
                    amps[pl.ds(pl.multiple_of(i * 256 + row, OJ), OJ), k * VB : (k + 1) * VB] = total
            return carry

        lax.fori_loop(0, 256 // OJ, place_rows, 0)

    turned = jnp.dot(amps[...], mirrored[...], preferred_element_type=F32).astype(BF)
    out[...] = (ladder[...].astype(F32) + turned.astype(F32)).astype(BF)


def add_turned(half, ids, shards, mirrored, ladder, previous):
    rows, pairs = 512, 8
    shard_spec = pl.BlockSpec((shards[0].shape[0], VB), lambda p: (0, 0))
    operands = [ids, *shards, mirrored, ladder]
    in_specs = (
        [pl.BlockSpec((256, 8), lambda p: (0, 0))]
        + [shard_spec] * 4
        + [
            pl.BlockSpec((NK * VB, 2 * VB), lambda p: (0, p)),
            pl.BlockSpec((rows, 2 * VB), lambda p: (half, p)),
        ]
    )
    aliases = {}
    if previous is not None:
        operands.append(previous)
        in_specs.append(pl.BlockSpec(memory_space=pl.ANY))
        aliases = {len(operands) - 1: 0}
    return pl.pallas_call(
        turn_kernel,
        grid=(pairs,),
        in_specs=in_specs,
        out_specs=pl.BlockSpec((rows, 2 * VB), lambda p: (half, p)),
        out_shape=jax.ShapeDtypeStruct((2 * rows, pairs * 2 * VB), BF),
        scratch_shapes=[pltpu.VMEM((rows, NK * VB), BF)],
        input_output_aliases=aliases,
        compiler_params=pltpu.CompilerParams(vmem_limit_bytes=48 * 2**20),
        cost_estimate=pl.CostEstimate(flops=45 * 10**8, bytes_accessed=16 * 2**20, transcendentals=0),
        name="add_turned",
    )(*operands)


def body(amplitudes, amp_ids, integrals, int_ids):
    z_groups = [[position(y, z, c) for z in range(NZ)] for y in range(NY) for c in range(NC)]
    along_z = lax.all_to_all(
        jnp.broadcast_to(integrals[None], (NZ,) + integrals.shape),
        "pair",
        0,
        0,
        axis_index_groups=z_groups,
    )
    along_y = [along_z] + [lax.ppermute(along_z, "pair", pair_shift(k, 0, 0)) for k in (1, 3, 2)]
    blocks = []
    for block in along_y:
        blocks += [block, lax.ppermute(block, "pair", pair_shift(0, 0, 1))]

    messages = jnp.swapaxes(amplitudes.reshape(4, 64, 8, VB), 0, 1).reshape(64, 32, VB)
    tile_ids = jnp.repeat(jnp.swapaxes(amp_ids, 0, 1).reshape(16, 8), 4, axis=0)
    tile_ids = jnp.pad(tile_ids.astype(BF)[:, None, :], ((0, 0), (0, 7), (0, VB - 8)))
    received = lax.all_to_all(jnp.concatenate([messages, tile_ids], axis=1), "pair", 0, 0)
    turned = jnp.swapaxes(received[:, :32].reshape(256, 8, VB), 0, 1).reshape(2, 1024, VB)
    turned_ids = jnp.transpose(received[:, 32, :8].reshape(256, 2)).reshape(4, VB)
    turned_ids = jnp.pad(turned_ids, ((0, 12), (0, 0)))

    own = jnp.swapaxes(amplitudes, 1, 2).reshape(2048, VB)
    own_ids = jnp.pad(amp_ids.astype(BF).reshape(1, VB), ((0, 15), (0, 0)))
    own_shards = virt_gather(jnp.concatenate([own, own_ids], axis=0))
    own_slots = jnp.concatenate([s[2048:2049] for s in own_shards], axis=0).astype(jnp.int32)

    first_shards = virt_gather(jnp.concatenate([turned[0], turned_ids], axis=0))
    second_shards = virt_gather(turned[1])
    slots = jnp.concatenate([s[1024:1028] for s in first_shards], axis=0).reshape(8, 256)
    slots = jnp.transpose(slots).astype(F32)

    place = lax.axis_index("pair").astype(jnp.int32)
    y, core = place // (NZ * NC), place % NC
    place = jnp.stack([y, (y + 3) % NY, (y + 1) % NY, (y + 2) % NY, core])
    mirror = jnp.asarray(mirror_matrices(), BF)
    ladder, mirrored = own_ladder(own_slots, int_ids, place, own_shards, blocks, mirror)
    out = add_turned(0, slots, first_shards, mirrored, ladder, None)
    out = add_turned(1, slots, second_shards, mirrored, ladder, out)
    return out.reshape(4, 256, 2048)


def solution(mesh):
    in_specs = (
        P("pair", None, "virt", None),
        P("pair", None, "virt"),
        P("virt", "pair", None),
        P("virt", None),
    )
    out_specs = P("pair", None, "virt")
    return jax.shard_map(body, mesh=mesh, in_specs=in_specs, out_specs=out_specs, check_vma=False)
```

```python
import functools

import jax
import jax.numpy as jnp
import numpy as np
from jax import lax
from jax.experimental import pallas as pl
from jax.experimental.pallas import tpu as pltpu
from jax.sharding import PartitionSpec as P

VB = 128
OJ = 16
NK = 16
NY, NZ, NC, NX = 4, 8, 2, 4
BF = jnp.bfloat16
F32 = jnp.float32


def position(y, z, c):
    return ((y % NY) * NZ + z % NZ) * NC + c % NC


def pair_shift(dy, dz, dc):
    return [
        (position(y, z, c), position(y + dy, z + dz, c + dc))
        for y in range(NY)
        for z in range(NZ)
        for c in range(NC)
    ]


def z_swap():
    return [
        (position(y, z, c), position(y, z ^ 1, c))
        for y in range(NY)
        for z in range(NZ)
        for c in range(NC)
    ]


def virt_shift(block, k):
    return lax.ppermute(block, "virt", [(x, (x + k) % NX) for x in range(NX)])


def mirror_matrix():
    matrix = np.zeros((2 * VB, 2 * VB), np.float32)
    for a in range(VB // 16):
        for e in range(16):
            even, odd = a * 16 + e, VB + e * (VB // 16) + a
            matrix[even, odd] = matrix[odd, even] = 1.0
    return matrix


def spread_rows(int_ids):
    place = lax.axis_index("pair").astype(jnp.int32)
    y, z, core = place // (NZ * NC), place // NC % NZ, place % NC
    at = jnp.arange(4 * NC * NZ, dtype=jnp.int32)
    y = (y + 4 - jnp.asarray([0, 1, 3, 2], jnp.int32)[at // 16]) % NY
    z = (z + 8 - jnp.asarray([0, 2, 6, 4], jnp.int32)[at // 2 % 4]) % NZ
    z = jnp.where(at % 2 == 0, z, z + 1 - 2 * (z % 2))
    core = jnp.where(at // NZ % 2 == 0, core, 1 - core)
    listed = y * 2 + z // 4
    chosen = (listed[:, None] == jnp.arange(8, dtype=jnp.int32)).astype(jnp.int32)
    tiles = jnp.sum(chosen[None] * int_ids[:, None, :], axis=-1)
    return tiles * VB + (z % 4 * 2 + core) * OJ


def params(mib):
    return pltpu.CompilerParams(vmem_limit_bytes=mib * 2**20)


def cost(flops, mib):
    return pl.CostEstimate(flops=flops, bytes_accessed=mib * 2**20, transcendentals=0)


VMEM = pl.BlockSpec(memory_space=pltpu.VMEM)
SMEM = pl.BlockSpec(memory_space=pltpu.SMEM)
ANY = pl.BlockSpec(memory_space=pl.ANY)


def dense_kernel(amp_ids, s0, s1, s2, s3, out, amps):
    shards = (s0, s1, s2, s3)

    def place_tiles(t, carry):
        i, jt = t // 16, t % 16
        amps[...] = jnp.zeros(amps.shape, BF)
        for n, shard in enumerate(shards):
            for s in range(2):
                k = amp_ids[n, t * 2 + s]
                source = pl.multiple_of((i * 2 + s) * 256 + jt * OJ, OJ)
                amps[:, pl.ds(pl.multiple_of(k * VB, VB), VB)] = shard[pl.ds(source, OJ), :]
        out[pl.ds(pl.multiple_of(t * OJ, OJ), OJ), :] = amps[:, : NK * VB]
        return carry

    lax.fori_loop(0, 64, place_tiles, 0)


def dense_own(amp_ids, shards):
    return pl.pallas_call(
        dense_kernel,
        in_specs=[SMEM] + [VMEM] * 4,
        out_specs=VMEM,
        out_shape=jax.ShapeDtypeStruct((1024, NK * VB), BF),
        scratch_shapes=[pltpu.VMEM((OJ, (NK + 1) * VB), BF)],
        compiler_params=params(48),
        cost_estimate=cost(0, 0),
        name="dense_own",
    )(amp_ids, *shards)


def columns(p):
    return pl.ds(pl.multiple_of(p * 2 * VB, 2 * VB), 2 * VB)


def own_kernel(rows, dense_own, *rest):
    blocks, ladder, spread, amps, zeros, dense, sums, sems = rest[:8], *rest[8:]
    fetch = pltpu.make_async_copy(dense_own, amps, sems.at[6])
    fetch.start()
    zeros[...] = jnp.zeros(zeros.shape, BF)

    def store_ladder(p, slot):
        return pltpu.make_async_copy(sums.at[slot], ladder.at[:, columns(p)], sems.at[slot])

    def store_spread(p, slot):
        return pltpu.make_async_copy(dense.at[slot], spread.at[:, columns(p)], sems.at[2 + slot])

    def clear(slot):
        return pltpu.make_async_copy(zeros, dense.at[slot], sems.at[4 + slot])

    clear(0).start()
    clear(1).start()

    def column_pair(p, carry):
        slot = p % 2
        clear(slot).wait()
        for half in range(2):
            b = p * 2 + half
            for n, block in enumerate(blocks):
                for at in range(NZ):
                    row = pl.multiple_of(rows[b, n * NZ + at], OJ)
                    dense[slot, pl.ds(row, OJ), half * VB : (half + 1) * VB] = block[at, b]
        store_spread(p, slot).start()

        @pl.when((p >= 1) & (p < 7))
        def _():
            store_spread(p - 1, 1 - slot).wait()
            clear(1 - slot).start()

        pl.when(p == 0)(fetch.wait)
        pl.when(p >= 2)(lambda: store_ladder(p - 2, slot).wait())
        sums[slot] = jnp.dot(amps[...], dense[slot], preferred_element_type=F32).astype(BF)
        store_ladder(p, slot).start()
        return carry

    lax.fori_loop(0, 8, column_pair, 0)
    for p in (6, 7):
        store_ladder(p, p % 2).wait()
        store_spread(p, p % 2).wait()


def own_ladder(rows, dense, blocks):
    return pl.pallas_call(
        own_kernel,
        in_specs=[SMEM, ANY] + [VMEM] * 8,
        out_specs=[ANY] * 2,
        out_shape=[
            jax.ShapeDtypeStruct((1024, 2048), BF),
            jax.ShapeDtypeStruct((NK * VB, 2048), BF),
        ],
        scratch_shapes=[
            pltpu.VMEM((1024, NK * VB), BF),
            pltpu.VMEM((NK * VB, 2 * VB), BF),
            pltpu.VMEM((2, NK * VB, 2 * VB), BF),
            pltpu.VMEM((2, 1024, 2 * VB), BF),
            pltpu.SemaphoreType.DMA((7,)),
        ],
        compiler_params=params(48),
        cost_estimate=cost(0, 0),
        name="own_ladder",
    )(rows, dense, *blocks)


def turn_kernel(ids, s0, s1, s2, s3, mirror, ladder, spread, out, amps, sums, owns, dense, sems):
    shards = (s0, s1, s2, s3)

    def store(p, slot):
        return pltpu.make_async_copy(sums.at[slot], out.at[:, columns(p)], sems.at[slot])

    def load_ladder(p, slot):
        return pltpu.make_async_copy(ladder.at[:, columns(p)], owns.at[slot], sems.at[2 + slot])

    def load_spread(p, slot):
        return pltpu.make_async_copy(spread.at[:, columns(p)], dense.at[slot], sems.at[4 + slot])

    for p in (0, 1):
        load_ladder(p, p).start()
        load_spread(p, p).start()

    def place_rows(t, carry):
        row = pl.multiple_of(t * OJ, OJ)
        slots = [
            jnp.broadcast_to(ids[pl.ds(row, OJ), n : n + 1], (OJ, VB)).astype(BF) for n in range(8)
        ]
        for i in range(4):
            values = [
                shards[n // 2][pl.ds(pl.multiple_of((i * 2 + n % 2) * 256 + row, OJ), OJ), :]
                for n in range(8)
            ]
            for k in range(NK):
                total = jnp.zeros((OJ, VB), BF)
                for n in range(8):
                    total = jnp.where(slots[n] == BF(k), values[n], total)
                amps[pl.ds(pl.multiple_of(i * 256 + row, OJ), OJ), k * VB : (k + 1) * VB] = total
        return carry

    lax.fori_loop(0, 256 // OJ, place_rows, 0)

    def column_pair(p, carry):
        slot = p % 2
        load_ladder(p, slot).wait()
        load_spread(p, slot).wait()
        pl.when(p >= 2)(lambda: store(p - 2, slot).wait())
        turned = jnp.dot(amps[...], dense[slot], preferred_element_type=F32).astype(BF)
        turned = jnp.dot(turned, mirror[...], preferred_element_type=F32)
        sums[slot] = (owns[slot].astype(F32) + turned).astype(BF)
        store(p, slot).start()

        @pl.when(p < 6)
        def _():
            load_ladder(p + 2, slot).start()
            load_spread(p + 2, slot).start()

        return carry

    lax.fori_loop(0, 8, column_pair, 0)
    store(6, 0).wait()
    store(7, 1).wait()


def add_turned(ids, shards, mirror, ladder, spread):
    return pl.pallas_call(
        turn_kernel,
        in_specs=[VMEM] * 6 + [ANY] * 2,
        out_specs=ANY,
        out_shape=jax.ShapeDtypeStruct((1024, 2048), BF),
        scratch_shapes=[
            pltpu.VMEM((1024, NK * VB), BF),
            pltpu.VMEM((2, 1024, 2 * VB), BF),
            pltpu.VMEM((2, 1024, 2 * VB), BF),
            pltpu.VMEM((2, NK * VB, 2 * VB), BF),
            pltpu.SemaphoreType.DMA((6,)),
        ],
        compiler_params=params(48),
        cost_estimate=cost(0, 0),
        name="add_turned",
    )(ids, *shards, mirror, ladder, spread)


def after(value, *others):
    return lax.optimization_barrier((value, *others))[0]


def body(amplitudes, amp_ids, integrals, int_ids):
    own = jnp.swapaxes(amplitudes, 1, 2).reshape(2048, VB)
    own_ids = jnp.pad(amp_ids.astype(BF).reshape(1, VB), ((0, 15), (0, 0)))
    own = jnp.concatenate([own, own_ids], axis=0)
    own_near = [virt_shift(own, k) for k in (1, 3)]

    swapped = lax.ppermute(integrals, "pair", z_swap())
    couple = jnp.stack([integrals, swapped])
    far = [lax.ppermute(couple, "pair", pair_shift(0, k, 0)) for k in (2, 6, 4)]
    along_z = jnp.concatenate([couple] + far)
    along_y = [along_z] + [lax.ppermute(along_z, "pair", pair_shift(k, 0, 0)) for k in (1, 3, 2)]

    messages = jnp.swapaxes(amplitudes.reshape(4, 64, 8, VB), 0, 1).reshape(64, 32, VB)
    tile_ids = jnp.repeat(jnp.swapaxes(amp_ids, 0, 1).reshape(16, 8), 4, axis=0)
    tile_ids = jnp.pad(tile_ids.astype(BF)[:, None, :], ((0, 0), (0, 7), (0, VB - 8)))
    messages = after(jnp.concatenate([messages, tile_ids], axis=1), *far)
    received = lax.all_to_all(messages, "pair", 0, 0)

    own_shards = [own, *own_near, virt_shift(own, 2)]
    own_slots = jnp.concatenate([s[2048:2049] for s in own_shards], axis=0).astype(jnp.int32)
    dense = dense_own(own_slots, own_shards)

    received = after(received, dense)
    turned = jnp.swapaxes(received[:, :32].reshape(256, 8, VB), 0, 1).reshape(2048, VB)
    turned_ids = jnp.transpose(received[:, 32, :8].reshape(256, 2)).reshape(4, VB)
    turned_ids = jnp.pad(turned_ids, ((0, 12), (0, 0)))
    turned = jnp.concatenate([turned, turned_ids], axis=0)
    shards = [turned] + [virt_shift(turned, k) for k in (1, 3, 2)]
    slots = jnp.concatenate([s[2048:2052] for s in shards], axis=0).reshape(8, 256)
    slots = jnp.transpose(slots).astype(F32)

    blocks = []
    for block in along_y:
        block = after(block, turned)
        blocks += [block, lax.ppermute(block, "pair", pair_shift(0, 0, 1))]

    ladder, spread = own_ladder(spread_rows(int_ids), dense, blocks)
    out = add_turned(slots, shards, jnp.asarray(mirror_matrix(), BF), ladder, spread)
    return out.reshape(4, 256, 2048)


def solution(mesh):
    in_specs = (
        P("pair", None, "virt", None),
        P("pair", None, "virt"),
        P("virt", "pair", None),
        P("virt", None),
    )
    out_specs = P("pair", None, "virt")
    return jax.shard_map(body, mesh=mesh, in_specs=in_specs, out_specs=out_specs, check_vma=False)
```

```python
import functools

import jax
import jax.numpy as jnp
import numpy as np
from jax import lax
from jax.experimental import pallas as pl
from jax.experimental.pallas import tpu as pltpu
from jax.sharding import PartitionSpec as P

VB = 128
OJ = 16
NK = 16
NY, NZ, NC, NX = 4, 8, 2, 4
BF = jnp.bfloat16
F32 = jnp.float32


def position(y, z, c):
    return ((y % NY) * NZ + z % NZ) * NC + c % NC


def pair_shift(dy, dz, dc):
    return [
        (position(y, z, c), position(y + dy, z + dz, c + dc))
        for y in range(NY)
        for z in range(NZ)
        for c in range(NC)
    ]


def virt_shift(block, k):
    return lax.ppermute(block, "virt", [(x, (x + k) % NX) for x in range(NX)])


def mirror_matrix():
    matrix = np.zeros((2 * VB, 2 * VB), np.float32)
    for a in range(VB // 16):
        for e in range(16):
            even, odd = a * 16 + e, VB + e * (VB // 16) + a
            matrix[even, odd] = matrix[odd, even] = 1.0
    return matrix


def spread_rows(int_ids):
    place = lax.axis_index("pair").astype(jnp.int32)
    y, core = place // (NZ * NC), place % NC
    at = jnp.arange(4 * NC * NZ, dtype=jnp.int32)
    y = (y + 4 - jnp.asarray([0, 1, 3, 2], jnp.int32)[at // 16]) % NY
    z = at % NZ
    core = jnp.where(at // NZ % 2 == 0, core, 1 - core)
    listed = y * 2 + z // 4
    chosen = (listed[:, None] == jnp.arange(8, dtype=jnp.int32)).astype(jnp.int32)
    tiles = jnp.sum(chosen[None] * int_ids[:, None, :], axis=-1)
    return tiles * VB + (z % 4 * 2 + core) * OJ


def params(mib):
    return pltpu.CompilerParams(vmem_limit_bytes=mib * 2**20)


def cost(flops, mib):
    return pl.CostEstimate(flops=flops, bytes_accessed=mib * 2**20, transcendentals=0)


VMEM = pl.BlockSpec(memory_space=pltpu.VMEM)
SMEM = pl.BlockSpec(memory_space=pltpu.SMEM)
ANY = pl.BlockSpec(memory_space=pl.ANY)


WIDE = 4 * VB


def columns(p):
    return pl.ds(pl.multiple_of(p * WIDE, WIDE), WIDE)


def own_kernel(rows, amp_ids, *rest):
    shards, blocks = rest[:4], rest[4:12]
    ladder, spread, amps, zeros, dense, sums, sems = rest[12:]
    zeros[...] = jnp.zeros(zeros.shape, BF)

    def store_ladder(p, slot):
        return pltpu.make_async_copy(sums.at[slot], ladder.at[:, columns(p)], sems.at[slot])

    def store_spread(p, slot):
        return pltpu.make_async_copy(dense.at[slot], spread.at[:, columns(p)], sems.at[2 + slot])

    def clear(slot):
        return pltpu.make_async_copy(zeros, dense.at[slot], sems.at[4 + slot])

    clear(0).start()
    clear(1).start()

    def place_tiles(t, carry):
        i, jt = t // 16, t % 16
        here = pl.ds(pl.multiple_of(t * OJ, OJ), OJ)
        amps[here, :] = jnp.zeros((OJ, amps.shape[1]), BF)
        for n, shard in enumerate(shards):
            for s in range(2):
                k = amp_ids[n, t * 2 + s]
                source = pl.multiple_of((i * 2 + s) * 256 + jt * OJ, OJ)
                amps[here, pl.ds(pl.multiple_of(k * VB, VB), VB)] = shard[pl.ds(source, OJ), :]
        return carry

    lax.fori_loop(0, 64, place_tiles, 0)

    def column_group(p, carry):
        slot = p % 2
        clear(slot).wait()
        for quarter in range(4):
            b = p * 4 + quarter
            for n, block in enumerate(blocks):
                for at in range(NZ):
                    row = pl.multiple_of(rows[b, n * NZ + at], OJ)
                    dense[slot, pl.ds(row, OJ), quarter * VB : (quarter + 1) * VB] = block[at, b]
        store_spread(p, slot).start()

        @pl.when((p >= 1) & (p < 3))
        def _():
            store_spread(p - 1, 1 - slot).wait()
            clear(1 - slot).start()

        pl.when(p >= 2)(lambda: store_ladder(p - 2, slot).wait())
        sums[slot] = jnp.dot(amps[:, : NK * VB], dense[slot], preferred_element_type=F32).astype(BF)
        store_ladder(p, slot).start()
        return carry

    lax.fori_loop(0, 4, column_group, 0)
    for p in (2, 3):
        store_ladder(p, p % 2).wait()
        store_spread(p, p % 2).wait()


def own_ladder(rows, amp_ids, shards, blocks):
    return pl.pallas_call(
        own_kernel,
        in_specs=[SMEM] * 2 + [VMEM] * 12,
        out_specs=[ANY] * 2,
        out_shape=[
            jax.ShapeDtypeStruct((1024, 2048), BF),
            jax.ShapeDtypeStruct((NK * VB, 2048), BF),
        ],
        scratch_shapes=[
            pltpu.VMEM((1024, (NK + 1) * VB), BF),
            pltpu.VMEM((NK * VB, WIDE), BF),
            pltpu.VMEM((2, NK * VB, WIDE), BF),
            pltpu.VMEM((2, 1024, WIDE), BF),
            pltpu.SemaphoreType.DMA((6,)),
        ],
        compiler_params=params(48),
        cost_estimate=cost(0, 0),
        name="own_ladder",
    )(rows, amp_ids, *shards, *blocks)


def turn_kernel(ids, s0, s1, s2, s3, mirror, ladder, spread, out, amps, sums, owns, dense, sems):
    shards = (s0, s1, s2, s3)

    def store(p, slot):
        return pltpu.make_async_copy(sums.at[slot], out.at[:, columns(p)], sems.at[slot])

    def load_ladder(p, slot):
        return pltpu.make_async_copy(ladder.at[:, columns(p)], owns.at[slot], sems.at[2 + slot])

    def load_spread(p, slot):
        return pltpu.make_async_copy(spread.at[:, columns(p)], dense.at[slot], sems.at[4 + slot])

    for p in (0, 1):
        load_ladder(p, p).start()
        load_spread(p, p).start()

    def place_rows(t, carry):
        row = pl.multiple_of(t * OJ, OJ)
        slots = [
            jnp.broadcast_to(ids[pl.ds(row, OJ), n : n + 1], (OJ, VB)).astype(BF) for n in range(8)
        ]
        for i in range(4):
            values = [
                shards[n // 2][pl.ds(pl.multiple_of((i * 2 + n % 2) * 256 + row, OJ), OJ), :]
                for n in range(8)
            ]
            for k in range(NK):
                total = jnp.zeros((OJ, VB), BF)
                for n in range(8):
                    total = jnp.where(slots[n] == BF(k), values[n], total)
                amps[pl.ds(pl.multiple_of(i * 256 + row, OJ), OJ), k * VB : (k + 1) * VB] = total
        return carry

    lax.fori_loop(0, 256 // OJ, place_rows, 0)

    def column_group(p, carry):
        slot = p % 2
        load_ladder(p, slot).wait()
        load_spread(p, slot).wait()
        pl.when(p >= 2)(lambda: store(p - 2, slot).wait())
        turned = jnp.dot(amps[...], dense[slot], preferred_element_type=F32).astype(BF)
        for pair in range(2):
            here = slice(pair * 2 * VB, (pair + 1) * 2 * VB)
            other = jnp.dot(turned[:, here], mirror[...], preferred_element_type=F32)
            sums[slot, :, here] = (owns[slot, :, here].astype(F32) + other).astype(BF)
        store(p, slot).start()

        @pl.when(p < 2)
        def _():
            load_ladder(p + 2, slot).start()
            load_spread(p + 2, slot).start()

        return carry

    lax.fori_loop(0, 4, column_group, 0)
    store(2, 0).wait()
    store(3, 1).wait()


def add_turned(ids, shards, mirror, ladder, spread):
    return pl.pallas_call(
        turn_kernel,
        in_specs=[VMEM] * 6 + [ANY] * 2,
        out_specs=ANY,
        out_shape=jax.ShapeDtypeStruct((1024, 2048), BF),
        scratch_shapes=[
            pltpu.VMEM((1024, NK * VB), BF),
            pltpu.VMEM((2, 1024, WIDE), BF),
            pltpu.VMEM((2, 1024, WIDE), BF),
            pltpu.VMEM((2, NK * VB, WIDE), BF),
            pltpu.SemaphoreType.DMA((6,)),
        ],
        compiler_params=params(48),
        cost_estimate=cost(0, 0),
        name="add_turned",
    )(ids, *shards, mirror, ladder, spread)


def after(value, *others):
    return lax.optimization_barrier((value, *others))[0]


def body(amplitudes, amp_ids, integrals, int_ids):
    own = jnp.swapaxes(amplitudes, 1, 2).reshape(2048, VB)
    own_ids = jnp.pad(amp_ids.astype(BF).reshape(1, VB), ((0, 15), (0, 0)))
    own = jnp.concatenate([own, own_ids], axis=0)
    own_near = [virt_shift(own, k) for k in (1, 3)]

    groups = [[position(y, z, c) for z in range(NZ)] for y in range(NY) for c in range(NC)]
    along_z = jnp.broadcast_to(integrals[None], (NZ,) + integrals.shape)
    along_z = lax.all_to_all(along_z, "pair", 0, 0, axis_index_groups=groups)
    beside = lax.ppermute(along_z, "pair", pair_shift(0, 0, 1))
    along_y = [along_z] + [lax.ppermute(along_z, "pair", pair_shift(k, 0, 0)) for k in (1, 3, 2)]

    messages = jnp.swapaxes(amplitudes.reshape(4, 64, 8, VB), 0, 1).reshape(64, 32, VB)
    tile_ids = jnp.repeat(jnp.swapaxes(amp_ids, 0, 1).reshape(16, 8), 4, axis=0)
    tile_ids = jnp.pad(tile_ids.astype(BF)[:, None, :], ((0, 0), (0, 7), (0, VB - 8)))
    messages = after(jnp.concatenate([messages, tile_ids], axis=1), along_z, *own_near)
    received = lax.all_to_all(messages, "pair", 0, 0)

    own_shards = [own, *own_near, virt_shift(after(own, beside), 2)]
    own_slots = jnp.concatenate([s[2048:2049] for s in own_shards], axis=0).astype(jnp.int32)

    turned = jnp.swapaxes(received[:, :32].reshape(256, 8, VB), 0, 1).reshape(2048, VB)
    turned_ids = jnp.transpose(received[:, 32, :8].reshape(256, 2)).reshape(4, VB)
    turned_ids = jnp.pad(turned_ids, ((0, 12), (0, 0)))
    turned = jnp.concatenate([turned, turned_ids], axis=0)
    shards = [turned] + [virt_shift(turned, k) for k in (1, 3, 2)]
    slots = jnp.concatenate([s[2048:2052] for s in shards], axis=0).reshape(8, 256)
    slots = jnp.transpose(slots).astype(F32)

    blocks = [along_z, beside]
    for block in along_y[1:]:
        block = after(block, turned) if block is along_y[2] or block is along_y[3] else block
        blocks += [block, lax.ppermute(block, "pair", pair_shift(0, 0, 1))]

    ladder, spread = own_ladder(spread_rows(int_ids), own_slots, own_shards, blocks)
    out = add_turned(slots, shards, jnp.asarray(mirror_matrix(), BF), ladder, spread)
    return out.reshape(4, 256, 2048)


def solution(mesh):
    in_specs = (
        P("pair", None, "virt", None),
        P("pair", None, "virt"),
        P("virt", "pair", None),
        P("virt", None),
    )
    out_specs = P("pair", None, "virt")
    return jax.shard_map(body, mesh=mesh, in_specs=in_specs, out_specs=out_specs, check_vma=False)
```

```python
import functools

import jax
import jax.numpy as jnp
import numpy as np
from jax import lax
from jax.experimental import pallas as pl
from jax.experimental.pallas import tpu as pltpu
from jax.sharding import PartitionSpec as P

VB = 128
OJ = 16
NK = 16
NY, NZ, NC, NX = 4, 8, 2, 4
BF = jnp.bfloat16
F32 = jnp.float32


def position(y, z, c):
    return ((y % NY) * NZ + z % NZ) * NC + c % NC


def pair_shift(dy, dz, dc):
    return [
        (position(y, z, c), position(y + dy, z + dz, c + dc))
        for y in range(NY)
        for z in range(NZ)
        for c in range(NC)
    ]


def virt_shift(block, k):
    return lax.ppermute(block, "virt", [(x, (x + k) % NX) for x in range(NX)])


def mirror_matrix():
    matrix = np.zeros((2 * VB, 2 * VB), np.float32)
    for a in range(VB // 16):
        for e in range(16):
            even, odd = a * 16 + e, VB + e * (VB // 16) + a
            matrix[even, odd] = matrix[odd, even] = 1.0
    return matrix


def spread_rows(int_ids):
    place = lax.axis_index("pair").astype(jnp.int32)
    y, core = place // (NZ * NC), place % NC
    at = jnp.arange(4 * NC * NZ, dtype=jnp.int32)
    y = (y + 4 - jnp.asarray([0, 1, 3, 2], jnp.int32)[at // 16]) % NY
    z = at % NZ
    core = jnp.where(at // NZ % 2 == 0, core, 1 - core)
    listed = y * 2 + z // 4
    chosen = (listed[:, None] == jnp.arange(8, dtype=jnp.int32)).astype(jnp.int32)
    tiles = jnp.sum(chosen[None] * int_ids[:, None, :], axis=-1)
    return tiles * VB + (z % 4 * 2 + core) * OJ


def params(mib):
    return pltpu.CompilerParams(vmem_limit_bytes=mib * 2**20)


def cost(flops, mib):
    return pl.CostEstimate(flops=flops, bytes_accessed=mib * 2**20, transcendentals=0)


VMEM = pl.BlockSpec(memory_space=pltpu.VMEM)
SMEM = pl.BlockSpec(memory_space=pltpu.SMEM)
ANY = pl.BlockSpec(memory_space=pl.ANY)


WIDE = 4 * VB


def columns(p):
    return pl.ds(pl.multiple_of(p * WIDE, WIDE), WIDE)


def own_kernel(rows, amp_ids, *rest):
    shards, blocks = rest[:4], rest[4:12]
    ladder, spread, amps, zeros, dense, sums, sems = rest[12:]
    zeros[...] = jnp.zeros(zeros.shape, BF)

    def store_ladder(p, slot):
        return pltpu.make_async_copy(sums.at[slot], ladder.at[:, columns(p)], sems.at[slot])

    def store_spread(p, slot):
        return pltpu.make_async_copy(dense.at[slot], spread.at[:, columns(p)], sems.at[2 + slot])

    def clear(slot):
        return pltpu.make_async_copy(zeros, dense.at[slot], sems.at[4 + slot])

    clear(0).start()
    clear(1).start()

    def place_tiles(t, carry):
        i, jt = t // 16, t % 16
        here = pl.ds(pl.multiple_of(t * OJ, OJ), OJ)
        amps[here, :] = jnp.zeros((OJ, amps.shape[1]), BF)
        for n, shard in enumerate(shards):
            for s in range(2):
                k = amp_ids[n, t * 2 + s]
                source = pl.multiple_of((i * 2 + s) * 256 + jt * OJ, OJ)
                amps[here, pl.ds(pl.multiple_of(k * VB, VB), VB)] = shard[pl.ds(source, OJ), :]
        return carry

    lax.fori_loop(0, 64, place_tiles, 0)

    def column_group(p, carry):
        slot = p % 2
        clear(slot).wait()
        for quarter in range(4):
            b = p * 4 + quarter
            for n, block in enumerate(blocks):
                for at in range(NZ):
                    row = pl.multiple_of(rows[b, n * NZ + at], OJ)
                    dense[slot, pl.ds(row, OJ), quarter * VB : (quarter + 1) * VB] = block[at, b]
        store_spread(p, slot).start()

        @pl.when((p >= 1) & (p < 3))
        def _():
            store_spread(p - 1, 1 - slot).wait()
            clear(1 - slot).start()

        pl.when(p >= 2)(lambda: store_ladder(p - 2, slot).wait())
        sums[slot] = jnp.dot(amps[:, : NK * VB], dense[slot], preferred_element_type=F32).astype(BF)
        store_ladder(p, slot).start()
        return carry

    lax.fori_loop(0, 4, column_group, 0)
    for p in (2, 3):
        store_ladder(p, p % 2).wait()
        store_spread(p, p % 2).wait()


def own_ladder(rows, amp_ids, shards, blocks):
    return pl.pallas_call(
        own_kernel,
        in_specs=[SMEM] * 2 + [VMEM] * 12,
        out_specs=[ANY] * 2,
        out_shape=[
            jax.ShapeDtypeStruct((1024, 2048), BF),
            jax.ShapeDtypeStruct((NK * VB, 2048), BF),
        ],
        scratch_shapes=[
            pltpu.VMEM((1024, (NK + 1) * VB), BF),
            pltpu.VMEM((NK * VB, WIDE), BF),
            pltpu.VMEM((2, NK * VB, WIDE), BF),
            pltpu.VMEM((2, 1024, WIDE), BF),
            pltpu.SemaphoreType.DMA((6,)),
        ],
        compiler_params=params(48),
        cost_estimate=cost(0, 0),
        name="own_ladder",
    )(rows, amp_ids, *shards, *blocks)


def turn_kernel(ids, s0, s1, s2, s3, mirror, ladder, spread, out, amps, sums, owns, dense, sems):
    shards = (s0, s1, s2, s3)

    def store(p, slot):
        return pltpu.make_async_copy(sums.at[slot], out.at[:, columns(p)], sems.at[slot])

    def load_ladder(p, slot):
        return pltpu.make_async_copy(ladder.at[:, columns(p)], owns.at[slot], sems.at[2 + slot])

    def load_spread(p, slot):
        return pltpu.make_async_copy(spread.at[:, columns(p)], dense.at[slot], sems.at[4 + slot])

    for p in (0, 1):
        load_ladder(p, p).start()
        load_spread(p, p).start()

    def place_rows(t, carry):
        row = pl.multiple_of(t * OJ, OJ)
        slots = [
            jnp.broadcast_to(ids[pl.ds(row, OJ), n : n + 1], (OJ, VB)).astype(BF) for n in range(8)
        ]
        for i in range(4):
            values = [
                shards[n // 2][pl.ds(pl.multiple_of((i * 2 + n % 2) * 256 + row, OJ), OJ), :]
                for n in range(8)
            ]
            for k in range(NK):
                total = jnp.zeros((OJ, VB), BF)
                for n in range(8):
                    total = jnp.where(slots[n] == BF(k), values[n], total)
                amps[pl.ds(pl.multiple_of(i * 256 + row, OJ), OJ), k * VB : (k + 1) * VB] = total
        return carry

    lax.fori_loop(0, 256 // OJ, place_rows, 0)

    def column_group(p, carry):
        slot = p % 2
        load_ladder(p, slot).wait()
        load_spread(p, slot).wait()
        pl.when(p >= 2)(lambda: store(p - 2, slot).wait())
        turned = jnp.dot(amps[...], dense[slot], preferred_element_type=F32).astype(BF)
        for pair in range(2):
            here = slice(pair * 2 * VB, (pair + 1) * 2 * VB)
            other = jnp.dot(turned[:, here], mirror[...], preferred_element_type=F32)
            sums[slot, :, here] = (owns[slot, :, here].astype(F32) + other).astype(BF)
        store(p, slot).start()

        @pl.when(p < 2)
        def _():
            load_ladder(p + 2, slot).start()
            load_spread(p + 2, slot).start()

        return carry

    lax.fori_loop(0, 4, column_group, 0)
    store(2, 0).wait()
    store(3, 1).wait()


def add_turned(ids, shards, mirror, ladder, spread):
    return pl.pallas_call(
        turn_kernel,
        in_specs=[VMEM] * 6 + [ANY] * 2,
        out_specs=ANY,
        out_shape=jax.ShapeDtypeStruct((1024, 2048), BF),
        scratch_shapes=[
            pltpu.VMEM((1024, NK * VB), BF),
            pltpu.VMEM((2, 1024, WIDE), BF),
            pltpu.VMEM((2, 1024, WIDE), BF),
            pltpu.VMEM((2, NK * VB, WIDE), BF),
            pltpu.SemaphoreType.DMA((6,)),
        ],
        compiler_params=params(48),
        cost_estimate=cost(0, 0),
        name="add_turned",
    )(ids, *shards, mirror, ladder, spread)


def after(value, *others):
    return lax.optimization_barrier((value, *others))[0]


def body(amplitudes, amp_ids, integrals, int_ids):
    own = jnp.swapaxes(amplitudes, 1, 2).reshape(2048, VB)
    own_ids = jnp.pad(amp_ids.astype(BF).reshape(1, VB), ((0, 15), (0, 0)))
    own = jnp.concatenate([own, own_ids], axis=0)
    own_near = [virt_shift(own, k) for k in (1, 3)]

    groups = [[position(y, z, c) for z in range(NZ)] for y in range(NY) for c in range(NC)]
    along_z = jnp.broadcast_to(integrals[None], (NZ,) + integrals.shape)
    along_z = lax.all_to_all(along_z, "pair", 0, 0, axis_index_groups=groups)
    beside = lax.ppermute(along_z, "pair", pair_shift(0, 0, 1))
    along_y = [along_z] + [lax.ppermute(along_z, "pair", pair_shift(k, 0, 0)) for k in (1, 3, 2)]

    messages = jnp.swapaxes(amplitudes.reshape(4, 64, 8, VB), 0, 1).reshape(64, 32, VB)
    tile_ids = jnp.repeat(jnp.swapaxes(amp_ids, 0, 1).reshape(16, 8), 4, axis=0)
    tile_ids = jnp.pad(tile_ids.astype(BF)[:, None, :], ((0, 0), (0, 7), (0, VB - 8)))
    messages = after(jnp.concatenate([messages, tile_ids], axis=1), along_z, *own_near, beside)
    received = lax.all_to_all(messages, "pair", 0, 0)

    own_shards = [own, *own_near, virt_shift(after(own, beside), 2)]
    own_slots = jnp.concatenate([s[2048:2049] for s in own_shards], axis=0).astype(jnp.int32)

    turned = jnp.swapaxes(received[:, :32].reshape(256, 8, VB), 0, 1).reshape(2048, VB)
    turned_ids = jnp.transpose(received[:, 32, :8].reshape(256, 2)).reshape(4, VB)
    turned_ids = jnp.pad(turned_ids, ((0, 12), (0, 0)))
    turned = jnp.concatenate([turned, turned_ids], axis=0)
    shards = [turned] + [virt_shift(turned, k) for k in (1, 3, 2)]
    slots = jnp.concatenate([s[2048:2052] for s in shards], axis=0).reshape(8, 256)
    slots = jnp.transpose(slots).astype(F32)

    blocks = [along_z, beside]
    for block in along_y[1:]:
        block = after(block, turned) if block is along_y[2] or block is along_y[3] else block
        blocks += [block, lax.ppermute(block, "pair", pair_shift(0, 0, 1))]

    ladder, spread = own_ladder(spread_rows(int_ids), own_slots, own_shards, blocks)
    out = add_turned(slots, shards, jnp.asarray(mirror_matrix(), BF), ladder, spread)
    return out.reshape(4, 256, 2048)


def solution(mesh):
    in_specs = (
        P("pair", None, "virt", None),
        P("pair", None, "virt"),
        P("virt", "pair", None),
        P("virt", None),
    )
    out_specs = P("pair", None, "virt")
    return jax.shard_map(body, mesh=mesh, in_specs=in_specs, out_specs=out_specs, check_vma=False)
```
